32 devices in a mesh: inp: 4 (over y, core), dep: 2 (over x), out: 4 (over z).
Axes of the slice: x: 2, y: 2, z: 4, core: 2. Of those that a mesh axis runs over, the one named last changes fastest.
Arguments:
- tokens: bfloat16 [1024, 16384], P('inp', 'out'), may hold values from -6 to 6
- gate_up_weight: bfloat16 [16384, 2, 28672], P('out', None, ('inp', 'dep')), may hold values from -0.046875 to 0.046875
- down_weight: bfloat16 [28672, 16384], P(('inp', 'dep'), 'out'), may hold values from -0.03125 to 0.03125
Outputs:
- layer_output: bfloat16 [1024, 16384], P(('inp', 'dep'), 'out')
The draws below stay inside these ranges and needn't reach their ends.
All inputs are finite; a program needn't handle non-finite values.
Results may differ from the reference program's by a relative error of at most 0.0049.
Values may be sent and summed in bfloat16 or wider, within the bound.
No kernel may reach another device: no remote copies, remote signals or barrier semaphores. Data moves between devices by JAX's collectives and lax.ppermute only.
A program may use at most 320 MiB of HBM per device.

```python
import jax
import jax.numpy as jnp

D = 16384
FF = 28672
TOKENS = 1024


def level_of(own_key, shape, split, smallest, high):
    loudness, own = 1.0, jax.random.fold_in(own_key, 6)
    for dim, shards_of in split:
        heights = jnp.exp(jax.random.uniform(jax.random.fold_in(own, dim), (shards_of,), jnp.float32, smallest / len(split), high / len(split)))
        loudness = loudness * jnp.repeat(heights, shape[dim] // shards_of).reshape([-1 if axis == dim else 1 for axis in range(len(shape))])
    return loudness


def gaussian(key, dims, width, most, split=(), dtype=jnp.bfloat16):
    values = width * jax.random.normal(key, dims, jnp.float32)
    if split:
        values = values * level_of(key, dims, split, -0.22, 0.18)
    return jnp.clip(values, -most, most).astype(dtype)


def setup_inputs(seed: int = 0) -> dict:
    streams_of = jax.random.split(jax.random.key(seed), 4)
    tokens = gaussian(streams_of[0], (TOKENS, D), 1.0, 6.0, ((0, 4), (1, 4)))
    gate_up_weight = gaussian(streams_of[1], (D, 2, FF), D ** -0.5, 0.046875, ((0, 4), (2, 8)))
    down_weight = gaussian(streams_of[2], (FF, D), FF ** -0.5, 0.03125, ((0, 8), (1, 4)))
    return dict(tokens=tokens, gate_up_weight=gate_up_weight, down_weight=down_weight)


def reference(tokens, gate_up_weight, down_weight):
    flat_weight = gate_up_weight.reshape(D, 2 * FF)
    projected = jnp.dot(tokens, flat_weight, preferred_element_type=jnp.float32)
    projected = projected.reshape(tokens.shape[0], 2, FF)
    hidden = (jax.nn.silu(projected[:, 0, :]) * projected[:, 1, :]).astype(jnp.bfloat16)
    result = jnp.dot(hidden, down_weight, preferred_element_type=jnp.float32)
    return result.astype(jnp.bfloat16)
```

```python
import functools

import jax
import jax.numpy as jnp
from jax import lax
from jax.experimental import pallas as pl
from jax.experimental.pallas import tpu as pltpu
from jax.sharding import PartitionSpec as P

STAGES = 4
PIECES = 4
LANES = 128
EARLY = 2
SPLITS = 2
VMEM_LIMIT = 16 * 2**20


def pieces_of(units):
    return max(n for n in range(1, PIECES + 1) if units % (LANES * n) == 0)


def flatten_kernel(weight_ref, flat_ref):
    rows, _, units = weight_ref.shape
    part = 32

    @pl.loop(0, rows // part)
    def _(step):
        block = pl.ds(pl.multiple_of(step * part, part), part)
        flat_ref[block, :] = weight_ref[block].reshape(part, 2 * units)


def flatten(weight, c, piece):
    width = weight.shape[0]
    rows = min(512, width)
    return pl.pallas_call(
        flatten_kernel,
        grid=(width // rows,),
        in_specs=[pl.BlockSpec((rows, 2, piece), lambda k: (k, 0, c))],
        out_specs=pl.BlockSpec((rows, 2 * piece), lambda k: (k, 0)),
        out_shape=jax.ShapeDtypeStruct((width, 2 * piece), weight.dtype),
        compiler_params=pltpu.CompilerParams(vmem_limit_bytes=VMEM_LIMIT),
        cost_estimate=pl.CostEstimate(
            flops=0, bytes_accessed=8 * width * piece, transcendentals=0
        ),
    )(weight)


def hop_kernel(side, line, sources, takes, sums, units, piece, names, *refs):
    refs = dict(zip(names, refs))
    here = lax.axis_index("out")
    devices = range(line) if side == 0 else range(line - 1, -1, -1)
    first, last = devices[0], devices[-1]
    own_units = 2 * piece * (sums == "send")
    came_units = 2 * piece * takes["sums"]

    def start(source, target, sem):
        pltpu.make_async_copy(source, target, refs["sems"].at[sem]).start()

    def wait(source, target, sem):
        pltpu.make_async_copy(source, target, refs["sems"].at[sem]).wait()

    rows = refs["total"].shape[0] if sums else 0
    if sums:
        for place, source in enumerate(sources):
            if source is not None:

                @pl.when(here == devices[place])
                def _():
                    start(refs["term%d" % source[0]].at[pl.ds(source[1], rows)], refs["own"], 0)

        if takes["sums"]:
            start(refs["came"].at[:, pl.ds(0, 2 * piece)], refs["running"], 1)
    if units:
        target = refs["sent"].at[:, pl.ds(own_units, piece)]

        @pl.when(here == first)
        def _():
            start(refs["fresh"], target, 2)

        @pl.when(here != first)
        def _():
            if takes["units"]:
                start(refs["came"].at[:, pl.ds(came_units, piece)], target, 2)
            else:
                start(refs["fresh"], target, 2)

    if sums:
        for place, source in enumerate(sources):

            @pl.when(here == devices[place])
            def _():
                if source is None:
                    refs["own"][...] = jnp.zeros_like(refs["own"])
                else:
                    wait(refs["term%d" % source[0]].at[pl.ds(source[1], rows)], refs["own"], 0)

        if takes["sums"]:
            wait(refs["came"].at[:, pl.ds(0, 2 * piece)], refs["running"], 1)

        part = 16

        @pl.loop(0, rows // part)
        def _(step):
            block = pl.ds(pl.multiple_of(step * part, part), part)
            total = refs["own"][block, :]
            if takes["sums"]:
                total = total + refs["running"][block, :].astype(jnp.float32)
            refs["own"][block, :] = total
            refs["total"][block, :] = total.astype(jnp.bfloat16)

        if sums == "send":
            start(refs["total"], refs["sent"].at[:, pl.ds(0, 2 * piece)], 3)
        if "done" in refs:

            @pl.when(here == last)
            def _():
                @pl.loop(0, rows // part)
                def _(step):
                    block = pl.ds(pl.multiple_of(step * part, part), part)
                    gate = refs["own"][block, pl.ds(0, piece)]
                    up = refs["own"][block, pl.ds(piece, piece)]
                    now = gate / (1.0 + jnp.exp(-gate)) * up
                    refs["finished"][block, :] = now.astype(jnp.bfloat16)

                start(refs["finished"], refs["done"], 4)
                wait(refs["finished"], refs["done"], 4)

        if sums == "send":
            wait(refs["total"], refs["sent"].at[:, pl.ds(0, 2 * piece)], 3)
    if units:
        wait(refs["fresh"], refs["sent"].at[:, pl.ds(own_units, piece)], 2)


def hop(side, line, came, fresh, terms, sources, takes, sums, units, done, piece, rows):
    names, inputs, out_names, outputs, scratch_names, scratch = [], [], [], [], [], []
    if came is not None:
        names.append("came")
        inputs.append(came)
    if units:
        names.append("fresh")
        inputs.append(fresh)
    for k, term in enumerate(terms):
        names.append("term%d" % k)
        inputs.append(term)
    width = piece * (2 * (sums == "send") + units)
    if width:
        out_names.append("sent")
        outputs.append(jax.ShapeDtypeStruct((rows, width), jnp.bfloat16))
    if done:
        out_names.append("done")
        outputs.append(jax.ShapeDtypeStruct((rows, piece), jnp.bfloat16))
    if sums:
        scratch_names += ["own", "running", "total", "finished"]
        scratch += [
            pltpu.VMEM((rows, 2 * piece), jnp.float32),
            pltpu.VMEM((rows, 2 * piece), jnp.bfloat16),
            pltpu.VMEM((rows, 2 * piece), jnp.bfloat16),
            pltpu.VMEM((rows, piece), jnp.bfloat16),
        ]
    scratch_names.append("sems")
    scratch.append(pltpu.SemaphoreType.DMA((5,)))
    hbm = pl.BlockSpec(memory_space=pltpu.HBM)
    out = pl.pallas_call(
        functools.partial(
            hop_kernel,
            side,
            line,
            sources,
            takes,
            sums,
            units,
            piece,
            names + out_names + scratch_names,
        ),
        in_specs=[hbm] * len(inputs),
        out_specs=[hbm] * len(outputs),
        out_shape=outputs,
        scratch_shapes=scratch,
        compiler_params=pltpu.CompilerParams(vmem_limit_bytes=VMEM_LIMIT // 2),
        cost_estimate=pl.CostEstimate(
            flops=10 * rows * piece, bytes_accessed=16 * rows * piece, transcendentals=rows * piece
        ),
    )(*inputs)
    out = dict(zip(out_names, out))
    return out.get("sent"), out.get("done")


def pick(entries, position):
    chosen = None
    for place, value in entries:
        chosen = value if chosen is None else jnp.where(position[place], value, chosen)
    return chosen


def halve(terms, axis, size, dim):
    index = lax.axis_index(axis)
    bit = 1
    while bit < size:
        shape = terms.shape
        cut = terms.reshape(*shape[:dim], shape[dim] // 2, 2, *shape[dim + 1 :])
        upper = (index // bit) % 2 == 1
        low = lax.index_in_dim(cut, 0, dim + 1, False)
        high = lax.index_in_dim(cut, 1, dim + 1, False)
        send = jnp.where(upper, low, high).astype(jnp.bfloat16)
        pairs = [(device, device ^ bit) for device in range(size)]
        came = lax.ppermute(send, axis, pairs).astype(jnp.float32)
        terms = jnp.where(upper, high, low) + came
        bit *= 2
    return jnp.squeeze(terms, dim)


def shards(mesh, tokens, gate_up_weight, down_weight):
    line, parts, groups = mesh.shape["out"], mesh.shape["dep"], mesh.shape["inp"]
    owners = groups * parts
    width = tokens.shape[1]
    own_rows = tokens.shape[0] // parts
    stage_rows = own_rows // STAGES
    units = gate_up_weight.shape[2]
    columns = pieces_of(units)
    piece = units // columns
    steps = STAGES * columns
    half = owners * stage_rows // 2
    out_width = down_weight.shape[1]

    here = lax.axis_index("out")
    places = [here == place for place in range(line)]
    hops = [
        [(place, place + 1) for place in range(line - 1)],
        [(place + 1, place) for place in range(line - 1)],
    ]

    split_tokens = tokens.reshape(parts, own_rows, width)
    rows = []
    for stage in range(STAGES):
        own = split_tokens[:, stage * stage_rows : (stage + 1) * stage_rows, :]
        own = own.reshape(parts * stage_rows, width)
        rows.append(lax.all_gather(own, "inp", axis=0, tiled=True))

    def after(value, *others):
        return lax.optimization_barrier((value, *others))[0]

    def term(number, flat, token):
        stage, c = divmod(number, columns)
        x = rows[stage] if token is None else after(rows[stage], token)
        return jnp.dot(x, flat[c], preferred_element_type=jnp.float32)

    early = min(EARLY, columns)
    flat = [flatten(gate_up_weight, c, piece) for c in range(early)]
    terms = [term(0, flat, None)]
    came, takes = [None, None], [dict(sums=False, units=False)] * 2
    fresh = [None, None]
    held = [dict(), dict()]
    delays = [line - 1, line]
    outs, results = [], []

    step = 0
    while len(results) < STAGES:
        work = []
        for side in range(2):
            back = 1 - side
            has_sums = step < steps + line - 1
            sums = "send" if step < steps + line - 2 else "end" if has_sums else ""
            age = step - delays[back]
            sends_units = 0 <= age < steps + line - 2
            if sends_units or sums:
                used, sources = [], [None] * line
                for place in range(line):
                    number = step - place
                    if has_sums and 0 <= number < steps:
                        known = [k for k, other in enumerate(used) if other is terms[number]]
                        if not known:
                            used.append(terms[number])
                        sources[place] = (known[0] if known else len(used) - 1, side * half)
                done = has_sums and step >= line - 1
                sent, mine = hop(
                    side,
                    line,
                    came[side],
                    fresh[back],
                    used,
                    sources,
                    takes[side],
                    sums,
                    sends_units,
                    done,
                    piece,
                    half,
                )
                if done:
                    fresh[side] = mine
            else:
                sent = None
            if sends_units:
                held[back][step] = sent[:, -piece:]
            elif takes[side]["units"]:
                held[back][step] = came[side][:, -piece:]
            came[side] = None
            if sent is not None:
                came[side] = lax.ppermute(sent, "out", hops[side])
                last = sent
            takes[side] = dict(sums=sums == "send", units=sends_units)
        if step + 1 < steps:
            if len(flat) < columns:
                flat.append(flatten(after(gate_up_weight, last), len(flat), piece))
            terms.append(term(step + 1, flat, last))
            work.append(terms[-1])
        stage = len(results)
        number = (stage + 1) * columns - 1
        if step >= number + 2 * line - 1:
            full = []
            for side in range(2):
                chunks = []
                for k in range(number - columns + 1, number + 1):
                    begin = k + delays[side]
                    ordered = places if side else places[::-1]
                    chunks.append(
                        pick([(p, held[side][begin + p]) for p in range(line)], ordered)
                    )
                full.append(jnp.concatenate(chunks, 1))
            full = jnp.concatenate(full, 0)
            final = stage == STAGES - 1
            totals = []
            for k in range(SPLITS):
                cut = slice(k * out_width // SPLITS, (k + 1) * out_width // SPLITS)
                out = jnp.dot(full, down_weight[:, cut], preferred_element_type=jnp.float32)
                work.append(out)
                if final:
                    out = out.reshape(groups, parts, stage_rows, out.shape[1])
                    totals.append(halve(halve(out, "inp", groups, 0), "dep", parts, 0))
                else:
                    totals.append(
                        lax.psum_scatter(out, ("inp", "dep"), scatter_dimension=0, tiled=True)
                    )
            results.append(jnp.concatenate(totals, 1).astype(jnp.bfloat16))
        if work and came[0] is not None:
            came[0] = after(came[0], *work)
        step += 1
    return jnp.concatenate(results, 0)


def solution(mesh):
    placed = (P("inp", "out"), P("out", None, ("inp", "dep")), P(("inp", "dep"), "out"))

    def run(tokens, gate_up_weight, down_weight):
        return shards(mesh, tokens, gate_up_weight, down_weight)

    return jax.shard_map(
        run, mesh=mesh, in_specs=placed, out_specs=P(("inp", "dep"), "out"), check_vma=False
    )
```

```python
import functools

import jax
import jax.numpy as jnp
from jax import lax
from jax.experimental import pallas as pl
from jax.experimental.pallas import tpu as pltpu
from jax.sharding import PartitionSpec as P

STAGES = 4
PIECES = 4
LANES = 128
EARLY = 1
VMEM_LIMIT = 16 * 2**20


def pieces_of(units):
    return max(n for n in range(1, PIECES + 1) if units % (LANES * n) == 0)


def flatten_kernel(weight_ref, flat_ref):
    rows, _, units = weight_ref.shape
    part = 32

    @pl.loop(0, rows // part)
    def _(step):
        block = pl.ds(pl.multiple_of(step * part, part), part)
        flat_ref[block, :] = weight_ref[block].reshape(part, 2 * units)


def flatten(weight, c, piece):
    width = weight.shape[0]
    rows = min(512, width)
    return pl.pallas_call(
        flatten_kernel,
        grid=(width // rows,),
        in_specs=[pl.BlockSpec((rows, 2, piece), lambda k: (k, 0, c))],
        out_specs=pl.BlockSpec((rows, 2 * piece), lambda k: (k, 0)),
        out_shape=jax.ShapeDtypeStruct((width, 2 * piece), weight.dtype),
        compiler_params=pltpu.CompilerParams(vmem_limit_bytes=VMEM_LIMIT),
        cost_estimate=pl.CostEstimate(
            flops=0, bytes_accessed=8 * width * piece, transcendentals=0
        ),
    )(weight)


def hop_kernel(side, line, sources, takes, sums, units, piece, names, *refs):
    refs = dict(zip(names, refs))
    here = lax.axis_index("out")
    devices = range(line) if side == 0 else range(line - 1, -1, -1)
    first, last = devices[0], devices[-1]
    own_units = 2 * piece * (sums == "send")
    came_units = 2 * piece * takes["sums"]

    def start(source, target, sem):
        pltpu.make_async_copy(source, target, refs["sems"].at[sem]).start()

    def wait(source, target, sem):
        pltpu.make_async_copy(source, target, refs["sems"].at[sem]).wait()

    rows = refs["total"].shape[0] if sums else 0
    if sums:
        for place, source in enumerate(sources):
            if source is not None:

                @pl.when(here == devices[place])
                def _():
                    start(refs["term%d" % source[0]].at[pl.ds(source[1], rows)], refs["own"], 0)

        if takes["sums"]:
            start(refs["came"].at[:, pl.ds(0, 2 * piece)], refs["running"], 1)
    if units:
        target = refs["sent"].at[:, pl.ds(own_units, piece)]

        @pl.when(here == first)
        def _():
            start(refs["fresh"], target, 2)

        @pl.when(here != first)
        def _():
            if takes["units"]:
                start(refs["came"].at[:, pl.ds(came_units, piece)], target, 2)
            else:
                start(refs["fresh"], target, 2)

    if sums:
        for place, source in enumerate(sources):

            @pl.when(here == devices[place])
            def _():
                if source is None:
                    refs["own"][...] = jnp.zeros_like(refs["own"])
                else:
                    wait(refs["term%d" % source[0]].at[pl.ds(source[1], rows)], refs["own"], 0)

        if takes["sums"]:
            wait(refs["came"].at[:, pl.ds(0, 2 * piece)], refs["running"], 1)

        part = 16

        @pl.loop(0, rows // part)
        def _(step):
            block = pl.ds(pl.multiple_of(step * part, part), part)
            total = refs["own"][block, :]
            if takes["sums"]:
                total = total + refs["running"][block, :].astype(jnp.float32)
            refs["own"][block, :] = total
            refs["total"][block, :] = total.astype(jnp.bfloat16)

        if sums == "send":
            start(refs["total"], refs["sent"].at[:, pl.ds(0, 2 * piece)], 3)
        if "done" in refs:

            @pl.when(here == last)
            def _():
                @pl.loop(0, rows // part)
                def _(step):
                    block = pl.ds(pl.multiple_of(step * part, part), part)
                    gate = refs["own"][block, pl.ds(0, piece)]
                    up = refs["own"][block, pl.ds(piece, piece)]
                    now = gate / (1.0 + jnp.exp(-gate)) * up
                    refs["finished"][block, :] = now.astype(jnp.bfloat16)

                start(refs["finished"], refs["done"], 4)
                wait(refs["finished"], refs["done"], 4)

        if sums == "send":
            wait(refs["total"], refs["sent"].at[:, pl.ds(0, 2 * piece)], 3)
    if units:
        wait(refs["fresh"], refs["sent"].at[:, pl.ds(own_units, piece)], 2)


def hop(side, line, came, fresh, terms, sources, takes, sums, units, done, piece, rows):
    names, inputs, out_names, outputs, scratch_names, scratch = [], [], [], [], [], []
    if came is not None:
        names.append("came")
        inputs.append(came)
    if units:
        names.append("fresh")
        inputs.append(fresh)
    for k, term in enumerate(terms):
        names.append("term%d" % k)
        inputs.append(term)
    width = piece * (2 * (sums == "send") + units)
    if width:
        out_names.append("sent")
        outputs.append(jax.ShapeDtypeStruct((rows, width), jnp.bfloat16))
    if done:
        out_names.append("done")
        outputs.append(jax.ShapeDtypeStruct((rows, piece), jnp.bfloat16))
    if sums:
        scratch_names += ["own", "running", "total", "finished"]
        scratch += [
            pltpu.VMEM((rows, 2 * piece), jnp.float32),
            pltpu.VMEM((rows, 2 * piece), jnp.bfloat16),
            pltpu.VMEM((rows, 2 * piece), jnp.bfloat16),
            pltpu.VMEM((rows, piece), jnp.bfloat16),
        ]
    scratch_names.append("sems")
    scratch.append(pltpu.SemaphoreType.DMA((5,)))
    hbm = pl.BlockSpec(memory_space=pltpu.HBM)
    out = pl.pallas_call(
        functools.partial(
            hop_kernel,
            side,
            line,
            sources,
            takes,
            sums,
            units,
            piece,
            names + out_names + scratch_names,
        ),
        in_specs=[hbm] * len(inputs),
        out_specs=[hbm] * len(outputs),
        out_shape=outputs,
        scratch_shapes=scratch,
        compiler_params=pltpu.CompilerParams(vmem_limit_bytes=VMEM_LIMIT // 2),
        cost_estimate=pl.CostEstimate(
            flops=10 * rows * piece, bytes_accessed=16 * rows * piece, transcendentals=rows * piece
        ),
    )(*inputs)
    out = dict(zip(out_names, out))
    return out.get("sent"), out.get("done")


def pick(entries, position):
    chosen = None
    for place, value in entries:
        chosen = value if chosen is None else jnp.where(position[place], value, chosen)
    return chosen


def halve(terms, axis, bit, size, dim):
    shape = terms.shape
    cut = terms.reshape(*shape[:dim], shape[dim] // 2, 2, *shape[dim + 1 :])
    upper = (lax.axis_index(axis) // bit) % 2 == 1
    low = lax.index_in_dim(cut, 0, dim + 1, False)
    high = lax.index_in_dim(cut, 1, dim + 1, False)
    send = jnp.where(upper, low, high).astype(jnp.bfloat16)
    pairs = [(device, device ^ bit) for device in range(size)]
    came = lax.ppermute(send, axis, pairs).astype(jnp.float32)
    return jnp.where(upper, high, low) + came


def scatter_last(terms, groups, parts):
    inp_bits = [1 << k for k in range(groups.bit_length() - 1)]
    dep_bits = [1 << k for k in range(parts.bit_length() - 1)]
    inp = [("inp", bit, groups, 0) for bit in inp_bits]
    dep = [("dep", bit, parts, 1) for bit in dep_bits]
    orders = [inp + dep, inp[:1] + dep + inp[1:]]
    cut = terms.shape[-1] // len(orders)
    halves = [terms[..., k * cut : (k + 1) * cut] for k in range(len(orders))]
    for moves in zip(*orders):
        halves = [halve(half, *move) for half, move in zip(halves, moves)]
        halves = list(lax.optimization_barrier(tuple(halves)))
    return jnp.concatenate([half[0, 0] for half in halves], 1)


def shards(mesh, tokens, gate_up_weight, down_weight):
    line, parts, groups = mesh.shape["out"], mesh.shape["dep"], mesh.shape["inp"]
    owners = groups * parts
    width = tokens.shape[1]
    own_rows = tokens.shape[0] // parts
    stage_rows = own_rows // STAGES
    units = gate_up_weight.shape[2]
    columns = pieces_of(units)
    piece = units // columns
    steps = STAGES * columns
    half = owners * stage_rows // 2
    out_width = down_weight.shape[1]

    here = lax.axis_index("out")
    places = [here == place for place in range(line)]
    hops = [
        [(place, place + 1) for place in range(line - 1)],
        [(place + 1, place) for place in range(line - 1)],
    ]

    split_tokens = tokens.reshape(parts, own_rows, width)
    rows = []
    for stage in range(STAGES):
        own = split_tokens[:, stage * stage_rows : (stage + 1) * stage_rows, :]
        own = own.reshape(parts * stage_rows, width)
        rows.append(lax.all_gather(own, "inp", axis=0, tiled=True))

    def after(value, *others):
        return lax.optimization_barrier((value, *others))[0]

    def term(number, flat, token):
        stage, c = divmod(number, columns)
        x = rows[stage] if token is None else after(rows[stage], token)
        return jnp.dot(x, flat[c], preferred_element_type=jnp.float32)

    early = min(EARLY, columns)
    flat = [flatten(gate_up_weight, c, piece) for c in range(early)]
    terms = [term(0, flat, None)]
    came, takes = [None, None], [dict(sums=False, units=False)] * 2
    fresh = [None, None]
    held = [dict(), dict()]
    delays = [line - 1, line]
    results = []

    trip = 2 * line - 1

    def chunk(side, k):
        ordered = places if side else places[::-1]
        begin = k + delays[side]
        return pick([(p, held[side][begin + p]) for p in range(line)], ordered)

    def chunks(first_chunk, end, *others):
        both = [[chunk(side, k) for k in range(first_chunk, end)] for side in range(2)]
        low, high = [jnp.concatenate(cut, 1) for cut in both]
        if others:
            low, high = after(low, *others), after(high, *others)
        return jnp.concatenate([low, high], 0)

    begins = [max((k + 1) * columns - 1 + trip, steps - 1) for k in range(STAGES - 1)]
    begins[0] = columns + trip
    begins[-1] = max(begins[-1], begins[-2] + 1)
    queue = list(enumerate(begins))
    waiting = []

    final = (STAGES - 1) * columns
    pending, total = final, None
    for step in range(steps + trip):
        work = []
        for side in range(2):
            back = 1 - side
            has_sums = step < steps + line - 1
            sums = "send" if step < steps + line - 2 else "end" if has_sums else ""
            age = step - delays[back]
            sends_units = 0 <= age < steps + line - 2
            if sends_units or sums:
                used, sources = [], [None] * line
                for place in range(line):
                    number = step - place
                    if has_sums and 0 <= number < steps:
                        known = [k for k, other in enumerate(used) if other is terms[number]]
                        if not known:
                            used.append(terms[number])
                        sources[place] = (known[0] if known else len(used) - 1, side * half)
                done = has_sums and step >= line - 1
                sent, mine = hop(
                    side,
                    line,
                    came[side],
                    fresh[back],
                    used,
                    sources,
                    takes[side],
                    sums,
                    sends_units,
                    done,
                    piece,
                    half,
                )
                if done:
                    fresh[side] = mine
            else:
                sent = None
            if sends_units:
                held[back][step] = sent[:, -piece:]
            elif takes[side]["units"]:
                held[back][step] = came[side][:, -piece:]
            came[side] = None
            if sent is not None:
                came[side] = lax.ppermute(sent, "out", hops[side])
                last = sent
            takes[side] = dict(sums=sums == "send", units=sends_units)
        if step + 1 < steps:
            if len(flat) < columns:
                flat.append(flatten(after(gate_up_weight, last), len(flat), piece))
            terms.append(term(step + 1, flat, last))
            work.append(terms[-1])
        for out in waiting:
            results.append(
                lax.psum_scatter(after(out, last), ("inp", "dep"), scatter_dimension=0, tiled=True)
            )
        waiting = []
        if queue and step >= queue[0][1]:
            stage, _ = queue.pop(0)
            full = chunks(stage * columns, (stage + 1) * columns, last)
            waiting.append(jnp.dot(full, down_weight, preferred_element_type=jnp.float32))
            work += waiting
        end = step - trip + 1
        if end > pending and (end - pending > 1 or end == steps or pending > final):
            cut = slice((pending - final) * piece, (end - final) * piece)
            out = jnp.dot(
                chunks(pending, end, *([last] if end < steps else [])),
                down_weight[cut],
                preferred_element_type=jnp.float32,
            )
            total = out if total is None else total + out
            pending = end
            work.append(total)
        if work and came[0] is not None:
            came[0] = after(came[0], *work)
    for out in waiting:
        results.append(lax.psum_scatter(out, ("inp", "dep"), scatter_dimension=0, tiled=True))
    total = total.reshape(groups, parts, stage_rows, out_width)
    results.append(scatter_last(total, groups, parts))
    return jnp.concatenate(results, 0).astype(jnp.bfloat16)


def solution(mesh):
    placed = (P("inp", "out"), P("out", None, ("inp", "dep")), P(("inp", "dep"), "out"))

    def run(tokens, gate_up_weight, down_weight):
        return shards(mesh, tokens, gate_up_weight, down_weight)

    return jax.shard_map(
        run, mesh=mesh, in_specs=placed, out_specs=P(("inp", "dep"), "out"), check_vma=False
    )
```

```python
import functools

import jax
import jax.numpy as jnp
from jax import lax
from jax.experimental import pallas as pl
from jax.experimental.pallas import tpu as pltpu
from jax.sharding import PartitionSpec as P

STAGES = 2
PIECES = 7
LANES = 128
LATE = 7
EARLY = 1
VMEM_LIMIT = 16 * 2**20


def pieces_of(units):
    return max(n for n in range(1, PIECES + 1) if units % (LANES * n) == 0)


def flatten_kernel(weight_ref, flat_ref):
    rows, _, units = weight_ref.shape
    part = 32

    @pl.loop(0, rows // part)
    def _(step):
        block = pl.ds(pl.multiple_of(step * part, part), part)
        flat_ref[block, :] = weight_ref[block].reshape(part, 2 * units)


def flatten(weight, c, piece):
    width = weight.shape[0]
    rows = min(512, width)
    return pl.pallas_call(
        flatten_kernel,
        grid=(width // rows,),
        in_specs=[pl.BlockSpec((rows, 2, piece), lambda k: (k, 0, c))],
        out_specs=pl.BlockSpec((rows, 2 * piece), lambda k: (k, 0)),
        out_shape=jax.ShapeDtypeStruct((width, 2 * piece), weight.dtype),
        compiler_params=pltpu.CompilerParams(vmem_limit_bytes=VMEM_LIMIT),
        cost_estimate=pl.CostEstimate(
            flops=0, bytes_accessed=8 * width * piece, transcendentals=0
        ),
    )(weight)


def hop_kernel(side, line, sources, takes, sums, units, piece, names, *refs):
    refs = dict(zip(names, refs))
    here = lax.axis_index("out")
    devices = range(line) if side == 0 else range(line - 1, -1, -1)
    first, last = devices[0], devices[-1]
    own_units = 2 * piece * (sums == "send")
    came_units = 2 * piece * takes["sums"]

    def start(source, target, sem):
        pltpu.make_async_copy(source, target, refs["sems"].at[sem]).start()

    def wait(source, target, sem):
        pltpu.make_async_copy(source, target, refs["sems"].at[sem]).wait()

    rows = refs["total"].shape[0] if sums else 0
    if sums:
        for place, source in enumerate(sources):
            if source is not None:

                @pl.when(here == devices[place])
                def _():
                    start(refs["term%d" % source[0]].at[pl.ds(source[1], rows)], refs["own"], 0)

        if takes["sums"]:
            start(refs["came"].at[:, pl.ds(0, 2 * piece)], refs["running"], 1)
    if units:
        target = refs["sent"].at[:, pl.ds(own_units, piece)]

        @pl.when(here == first)
        def _():
            start(refs["fresh"], target, 2)

        @pl.when(here != first)
        def _():
            if takes["units"]:
                start(refs["came"].at[:, pl.ds(came_units, piece)], target, 2)
            else:
                start(refs["fresh"], target, 2)

    if sums:
        for place, source in enumerate(sources):

            @pl.when(here == devices[place])
            def _():
                if source is None:
                    refs["own"][...] = jnp.zeros_like(refs["own"])
                else:
                    wait(refs["term%d" % source[0]].at[pl.ds(source[1], rows)], refs["own"], 0)

        if takes["sums"]:
            wait(refs["came"].at[:, pl.ds(0, 2 * piece)], refs["running"], 1)

        part = 16

        @pl.loop(0, rows // part)
        def _(step):
            block = pl.ds(pl.multiple_of(step * part, part), part)
            total = refs["own"][block, :]
            if takes["sums"]:
                total = total + refs["running"][block, :].astype(jnp.float32)
            refs["own"][block, :] = total
            refs["total"][block, :] = total.astype(jnp.bfloat16)

        if sums == "send":
            start(refs["total"], refs["sent"].at[:, pl.ds(0, 2 * piece)], 3)
        if "done" in refs:

            @pl.when(here == last)
            def _():
                @pl.loop(0, rows // part)
                def _(step):
                    block = pl.ds(pl.multiple_of(step * part, part), part)
                    gate = refs["own"][block, pl.ds(0, piece)]
                    up = refs["own"][block, pl.ds(piece, piece)]
                    now = gate / (1.0 + jnp.exp(-gate)) * up
                    refs["finished"][block, :] = now.astype(jnp.bfloat16)

                start(refs["finished"], refs["done"], 4)
                wait(refs["finished"], refs["done"], 4)

        if sums == "send":
            wait(refs["total"], refs["sent"].at[:, pl.ds(0, 2 * piece)], 3)
    if units:
        wait(refs["fresh"], refs["sent"].at[:, pl.ds(own_units, piece)], 2)


def hop(side, line, came, fresh, terms, sources, takes, sums, units, done, piece, rows):
    names, inputs, out_names, outputs, scratch_names, scratch = [], [], [], [], [], []
    if came is not None:
        names.append("came")
        inputs.append(came)
    if units:
        names.append("fresh")
        inputs.append(fresh)
    for k, term in enumerate(terms):
        names.append("term%d" % k)
        inputs.append(term)
    width = piece * (2 * (sums == "send") + units)
    if width:
        out_names.append("sent")
        outputs.append(jax.ShapeDtypeStruct((rows, width), jnp.bfloat16))
    if done:
        out_names.append("done")
        outputs.append(jax.ShapeDtypeStruct((rows, piece), jnp.bfloat16))
    if sums:
        scratch_names += ["own", "running", "total", "finished"]
        scratch += [
            pltpu.VMEM((rows, 2 * piece), jnp.float32),
            pltpu.VMEM((rows, 2 * piece), jnp.bfloat16),
            pltpu.VMEM((rows, 2 * piece), jnp.bfloat16),
            pltpu.VMEM((rows, piece), jnp.bfloat16),
        ]
    scratch_names.append("sems")
    scratch.append(pltpu.SemaphoreType.DMA((5,)))
    hbm = pl.BlockSpec(memory_space=pltpu.HBM)
    out = pl.pallas_call(
        functools.partial(
            hop_kernel,
            side,
            line,
            sources,
            takes,
            sums,
            units,
            piece,
            names + out_names + scratch_names,
        ),
        in_specs=[hbm] * len(inputs),
        out_specs=[hbm] * len(outputs),
        out_shape=outputs,
        scratch_shapes=scratch,
        compiler_params=pltpu.CompilerParams(vmem_limit_bytes=VMEM_LIMIT // 2),
        cost_estimate=pl.CostEstimate(
            flops=10 * rows * piece, bytes_accessed=16 * rows * piece, transcendentals=rows * piece
        ),
    )(*inputs)
    out = dict(zip(out_names, out))
    return out.get("sent"), out.get("done")


def pick(entries, position):
    chosen = None
    for place, value in entries:
        chosen = value if chosen is None else jnp.where(position[place], value, chosen)
    return chosen


def swap(block, bit, size):
    pairs = [(device, device ^ bit) for device in range(size)]
    return lax.ppermute(block, "inp", pairs)


def join(block, bit, size):
    other = swap(block, bit, size)
    upper = (lax.axis_index("inp") // bit) % 2 == 1
    low, high = jnp.where(upper, other, block), jnp.where(upper, block, other)
    return jnp.concatenate([low, high], 0)


def halve(terms, axis, bit, size, dim):
    shape = terms.shape
    cut = terms.reshape(*shape[:dim], shape[dim] // 2, 2, *shape[dim + 1 :])
    upper = (lax.axis_index(axis) // bit) % 2 == 1
    low = lax.index_in_dim(cut, 0, dim + 1, False)
    high = lax.index_in_dim(cut, 1, dim + 1, False)
    send = jnp.where(upper, low, high).astype(jnp.bfloat16)
    pairs = [(device, device ^ bit) for device in range(size)]
    came = lax.ppermute(send, axis, pairs).astype(jnp.float32)
    return jnp.where(upper, high, low) + came


def scatter_last(terms, groups, parts):
    inp_bits = [1 << k for k in range(groups.bit_length() - 1)]
    dep_bits = [1 << k for k in range(parts.bit_length() - 1)]
    inp = [("inp", bit, groups, 0) for bit in inp_bits]
    dep = [("dep", bit, parts, 1) for bit in dep_bits]
    orders = [inp + dep, inp[:1] + dep + inp[1:]]
    cut = terms.shape[-1] // len(orders)
    halves = [terms[..., k * cut : (k + 1) * cut] for k in range(len(orders))]
    for moves in zip(*orders):
        halves = [halve(half, *move) for half, move in zip(halves, moves)]
        halves = list(lax.optimization_barrier(tuple(halves)))
    return jnp.concatenate([half[0, 0] for half in halves], 1)


def shards(mesh, tokens, gate_up_weight, down_weight):
    line, parts, groups = mesh.shape["out"], mesh.shape["dep"], mesh.shape["inp"]
    owners = groups * parts
    width = tokens.shape[1]
    own_rows = tokens.shape[0] // parts
    stage_rows = own_rows // STAGES
    units = gate_up_weight.shape[2]
    columns = pieces_of(units)
    piece = units // columns
    steps = STAGES * columns
    half = owners * stage_rows // 2
    out_width = down_weight.shape[1]

    here = lax.axis_index("out")
    places = [here == place for place in range(line)]
    hops = [
        [(place, place + 1) for place in range(line - 1)],
        [(place + 1, place) for place in range(line - 1)],
    ]

    split_tokens = tokens.reshape(parts, own_rows, width)
    own = [
        split_tokens[:, k * stage_rows : (k + 1) * stage_rows, :].reshape(-1, width)
        for k in range(STAGES)
    ]
    near, far = own[0], swap(own[0], groups // 2, groups)
    bit = 1
    while bit < groups // 2:
        near, far = join(near, bit, groups), join(far, bit, groups)
        bit *= 2
    rows = [jnp.concatenate([near, far], 0)]
    for stage in range(1, STAGES):
        rows.append(lax.all_gather(own[stage], "inp", axis=0, tiled=True))

    def after(value, *others):
        return lax.optimization_barrier((value, *others))[0]

    def term(number, flat, token):
        stage, c = divmod(number, columns)
        if number == 0:
            both = [
                jnp.dot(x, flat[c], preferred_element_type=jnp.float32) for x in (near, far)
            ]
            return [(both[0], 0), (both[1], 0)]
        x = rows[stage] if token is None else after(rows[stage], token)
        product = jnp.dot(x, flat[c], preferred_element_type=jnp.float32)
        return [(product, 0), (product, half)]

    early = min(EARLY, columns)
    flat = [flatten(gate_up_weight, c, piece) for c in range(early)]
    terms = [term(0, flat, None)]
    came, takes = [None, None], [dict(sums=False, units=False)] * 2
    fresh = [None, None]
    held = [dict(), dict()]
    delays = [line - 1, line]
    results = []

    trip = 2 * line - 1

    def chunk(side, k):
        ordered = places if side else places[::-1]
        begin = k + delays[side]
        return pick([(p, held[side][begin + p]) for p in range(line)], ordered)

    def chunks(first_chunk, end, *others):
        both = [[chunk(side, k) for k in range(first_chunk, end)] for side in range(2)]
        low, high = [jnp.concatenate(cut, 1) for cut in both]
        if first_chunk < columns:
            upper = lax.axis_index("inp") >= groups // 2
            low, high = jnp.where(upper, high, low), jnp.where(upper, low, high)
        if others:
            low, high = after(low, *others), after(high, *others)
        return jnp.concatenate([low, high], 0)

    begins = [max((k + 1) * columns - 1 + trip, steps - 1) for k in range(STAGES - 1)]
    begins = [begin + k for k, begin in enumerate(begins)]
    queue = list(enumerate(begins))
    waiting = []

    final = (STAGES - 1) * columns
    pending, total = final, None
    for step in range(steps + trip):
        work = []
        for side in range(2):
            back = 1 - side
            has_sums = step < steps + line - 1
            sums = "send" if step < steps + line - 2 else "end" if has_sums else ""
            age = step - delays[back]
            sends_units = 0 <= age < steps + line - 2
            if sends_units or sums:
                used, sources = [], [None] * line
                for place in range(line):
                    number = step - place
                    if has_sums and 0 <= number < steps:
                        array, first_row = terms[number][side]
                        sources[place] = (len(used), first_row)
                        used.append(array)
                done = has_sums and step >= line - 1
                sent, mine = hop(
                    side,
                    line,
                    came[side],
                    fresh[back],
                    used,
                    sources,
                    takes[side],
                    sums,
                    sends_units,
                    done,
                    piece,
                    half,
                )
                if done:
                    fresh[side] = mine
            else:
                sent = None
            if sends_units:
                held[back][step] = sent[:, -piece:]
            elif takes[side]["units"]:
                held[back][step] = came[side][:, -piece:]
            came[side] = None
            if sent is not None:
                came[side] = lax.ppermute(sent, "out", hops[side])
                last = sent
            takes[side] = dict(sums=sums == "send", units=sends_units)
        if step + 1 < steps:
            if len(flat) < columns:
                flat.append(flatten(after(gate_up_weight, last), len(flat), piece))
            terms.append(term(step + 1, flat, last))
            work.append(terms[-1][0][0])
        for out in waiting:
            results.append(
                lax.psum_scatter(after(out, last), ("inp", "dep"), scatter_dimension=0, tiled=True)
            )
        waiting = []
        if queue and step >= queue[0][1]:
            stage, _ = queue.pop(0)
            full = chunks(stage * columns, (stage + 1) * columns, last)
            waiting.append(jnp.dot(full, down_weight, preferred_element_type=jnp.float32))
            work += waiting
        end = step - trip + 1
        if end > pending and end in (steps - LATE, steps):
            cut = slice((pending - final) * piece, (end - final) * piece)
            out = jnp.dot(
                chunks(pending, end, *([last] if end < steps else [])),
                down_weight[cut],
                preferred_element_type=jnp.float32,
            )
            total = out if total is None else total + out
            pending = end
            work.append(total)
        if work and came[0] is not None:
            came[0] = after(came[0], *work)
    for out in waiting:
        results.append(lax.psum_scatter(out, ("inp", "dep"), scatter_dimension=0, tiled=True))
    total = total.reshape(groups, parts, stage_rows, out_width)
    results.append(scatter_last(total, groups, parts))
    return jnp.concatenate(results, 0).astype(jnp.bfloat16)


def solution(mesh):
    placed = (P("inp", "out"), P("out", None, ("inp", "dep")), P(("inp", "dep"), "out"))

    def run(tokens, gate_up_weight, down_weight):
        return shards(mesh, tokens, gate_up_weight, down_weight)

    return jax.shard_map(
        run, mesh=mesh, in_specs=placed, out_specs=P(("inp", "dep"), "out"), check_vma=False
    )
```
